32 devices in a mesh: space: 8 (over z, x), member: 4 (over y, core).
Axes of the slice: x: 2, y: 2, z: 4, core: 2. Of those that a mesh axis runs over, the one named last changes fastest.
Arguments:
- state: float32 [32, 49152], P(None, 'space'), may hold values from -6 to 6
- ensemble: bfloat16 [4, 32, 49152], P('member', None, 'space'), may hold values from -6 to 6
- vertical: bfloat16 [32, 32], replicated, may hold values from -1 to 1
- coords: int32 [2, 49152], P(None, 'space'), may hold values from 0 to 6143, as said below
- pairs: int32 [2, 1920], P(None, 'space'), may hold values from 0 to 51, as said below
- pair_count: int32 [8], P('space'), may hold values from 60 to 240, as said below
Outputs:
- first: float32 [32, 49152], P(None, 'space')
- second: float32 [32, 49152], P(None, 'space')
The draws below stay inside these ranges and needn't reach their ends.
Inputs may be any that keep to these rules, and one draw needn't show every extreme that they name: `coords`: row 0 is a position on a periodic strip of 6144 positions: column g lies 0 to 47 positions ahead of g // 8, periodically; row 1 lies in 0 to 31. Each tile's 240 slots hold distinct pairs; the destination is 0 to 47 and the source lies from the destination to the destination + 4. Only the first pair_count[t] slots of tile t are live.
All inputs are finite; a program needn't handle non-finite values.
Results may differ from the reference program's by a relative error of at most 0.0057.
Values may be sent and summed in bfloat16 or wider, within the bound.
A program may use at most 64 MiB of HBM per device.

```python
import jax
import jax.numpy as jnp
from jax import lax

LEV = 32
BLOCK = 128
REACH = 2
BLK_DEV = 48
TILES = 8
COLS = 49152
MAXP = 240
MEMBERS = 4


def draw_coords(key, part):
    key = jax.random.fold_in(key, 11)
    key_a, key_b = jax.random.split(key)
    column = jnp.arange(COLS, dtype=jnp.int32)
    jitter = jax.random.randint(key_a, (COLS,), 0, 48)
    jitter = jnp.where(column == 0, 0, jnp.where(column == COLS - 1, 0, jitter))
    along = (column // 8 + jitter) % (COLS // 8)
    across = jax.random.randint(key_b, (COLS,), 0, 32)
    return jnp.stack([along, across]).astype(jnp.int32)


def draw_pairs(key, part):
    key = jax.random.fold_in(key, 23)
    keys = jax.random.split(key, TILES)
    orders = jax.vmap(lambda single: jax.random.permutation(single, MAXP))(keys)
    span = 2 * REACH + 1
    target = orders // span
    source = target + orders % span
    return jnp.stack([target.reshape(-1), source.reshape(-1)]).astype(jnp.int32)


def draw_pair_count(key, part):
    key = jax.random.fold_in(key, 37)
    key_a, key_b = jax.random.split(key)
    ranking = jax.random.permutation(key_a, TILES)
    base = jax.random.randint(key_b, (TILES,), MAXP // 4, 2 * MAXP // 3 + 1)
    counted = jnp.where(ranking < max(1, TILES // 16), MAXP, base)
    counted = jnp.where(ranking == TILES - 1, MAXP // 4, counted)
    return counted.astype(jnp.int32)


def shard_levels(stream_key, shape, cuts, smallest, high):
    def one(dim, parts):
        steps = jax.random.uniform(jax.random.fold_in(jax.random.fold_in(stream_key, 6), dim), (parts,), jnp.float32, smallest / len(cuts), high / len(cuts))
        return jnp.repeat(jnp.exp(steps), shape[dim] // parts).reshape((-1,) + (1,) * (len(shape) - dim - 1))

    loudness = one(*cuts[0])
    for cut in cuts[1:]:
        loudness = loudness * one(*cut)
    return loudness


def scatter_about(rng, shape, scale, bound, pieces=(), kind=jnp.bfloat16):
    array = jax.random.normal(rng, shape, jnp.float32) * scale
    if len(pieces) > 0:
        array = shard_levels(rng, shape, pieces, -0.22, 0.18) * array
    return jnp.clip(array, min=-bound, max=bound).astype(kind)


def setup_inputs(seed: int = 0) -> dict:
    key_list = jax.random.split(jax.random.key(seed), 7)
    return {
        "state": scatter_about(key_list[0], (LEV, COLS), 1.0, 6.0, ((1, 8),), jnp.float32),
        "ensemble": scatter_about(key_list[1], (MEMBERS, LEV, COLS), 1.0, 6.0, ((0, 4), (2, 8))),
        "vertical": scatter_about(key_list[2], (LEV, LEV), LEV ** -0.5, 1.0),
        "coords": draw_coords(jax.random.fold_in(key_list[6], 71), 0),
        "pairs": draw_pairs(jax.random.fold_in(key_list[6], 71), 0),
        "pair_count": draw_pair_count(jax.random.fold_in(key_list[6], 71), 0),
    }


scale_len = 4.0

def gaspari(r):
    near = (((-0.25 * r + 0.5) * r + 0.625) * r - 5.0 / 3.0) * r * r + 1.0
    rf = jnp.maximum(r, 1.0)
    far = ((((rf / 12.0 - 0.5) * rf + 0.625) * rf + 5.0 / 3.0) * rf - 5.0) * rf + 4.0 - 2.0 / (3.0 * rf)
    return jnp.where(r <= 1.0, near, jnp.where(r < 2.0, far, jnp.zeros_like(r)))

def pair_weights(src_xy, dst_xy, period):
    along = jnp.abs(src_xy[0][:, :, None] - dst_xy[0][:, None, :])
    along = jnp.minimum(along, period - along)
    across = jnp.abs(src_xy[1][:, :, None] - dst_xy[1][:, None, :])
    dist = jnp.sqrt((along * along + across * across).astype(jnp.float32))
    return gaspari(dist / scale_len).astype(jnp.bfloat16)

def reference(state, ensemble, vertical, coords, pairs, pair_count):
    cols_dev = BLK_DEV * BLOCK
    width = REACH * BLOCK
    total = cols_dev * TILES
    period = total // 8
    ext_blocks = BLK_DEV + 2 * REACH
    pair_tiles = pairs.reshape(2, TILES, MAXP)

    def apply(field):
        schur = (ensemble.astype(jnp.float32) * field[None]).astype(jnp.bfloat16)
        flat = schur.transpose(1, 0, 2).reshape(LEV, MEMBERS * total)
        lifted = jnp.dot(vertical, flat, preferred_element_type=jnp.float32).astype(jnp.bfloat16)
        lifted = lifted.reshape(LEV, MEMBERS, total).transpose(1, 0, 2)

        def tile(t):
            idx = (t * cols_dev - width + jnp.arange(cols_dev + 2 * width, dtype=jnp.int32)) % total
            ext = jnp.take(lifted, idx, axis=2)
            xy_ext = jnp.take(coords, idx, axis=1)
            xy = lax.dynamic_slice_in_dim(coords, (t * cols_dev).astype(jnp.int32), cols_dev, 1)
            dst = pair_tiles[0][t]
            src = pair_tiles[1][t]
            count = pair_count[t]
            weights = pair_weights(xy_ext.reshape(2, ext_blocks, BLOCK)[:, src], xy.reshape(2, BLK_DEV, BLOCK)[:, dst], period)
            picked = ext.reshape(MEMBERS, LEV, ext_blocks, BLOCK)[:, :, src]
            contrib = jnp.einsum('mlpc,pcd->pmld', picked.astype(jnp.float32), weights.astype(jnp.float32))
            live = (jnp.arange(MAXP, dtype=jnp.int32) < count).astype(jnp.float32)
            select = (dst[:, None] == jnp.arange(BLK_DEV, dtype=jnp.int32)[None, :]).astype(jnp.float32) * live[:, None]
            spread = jnp.einsum('pb,pmld->mlbd', select, contrib, precision=lax.Precision.HIGHEST)
            spread = spread.reshape(MEMBERS, LEV, cols_dev)
            member_x = lax.dynamic_slice_in_dim(ensemble, (t * cols_dev).astype(jnp.int32), cols_dev, 2).astype(jnp.float32)
            return lax.optimization_barrier(jnp.sum(member_x * spread, axis=0)) / (MEMBERS - 1)
        out = lax.map(tile, jnp.arange(TILES, dtype=jnp.int32))
        return out.transpose(1, 0, 2).reshape(LEV, total)
    first = apply(state)
    second = apply(first)
    return (first, second)
```

```python
import functools

import jax
import jax.numpy as jnp
from jax import lax
from jax.experimental import pallas as pl
from jax.experimental.pallas import tpu as pltpu
from jax.sharding import PartitionSpec as P

BLOCK = 128
REACH = 2
SCALE = 4.0
HALO = REACH * BLOCK
FAR = 131072.0
MESH = pl.DeviceIdType.MESH


def gaspari(r):
    near = (((-0.25 * r + 0.5) * r + 0.625) * r - 5.0 / 3.0) * r * r + 1.0
    rf = jnp.maximum(r, 1.0)
    far = (
        ((((rf / 12.0 - 0.5) * rf + 0.625) * rf + 5.0 / 3.0) * rf - 5.0) * rf
        + 4.0
        - 2.0 / (3.0 * rf)
    )
    return jnp.where(r <= 1.0, near, jnp.where(r < 2.0, far, jnp.zeros_like(r)))


def iota(shape, dim):
    return lax.broadcasted_iota(jnp.int32, shape, dim)


def dot(a, b):
    return jnp.dot(a, b, preferred_element_type=jnp.float32)


def kernel(
    tiles, members, blocks_dev, group,
    state, ens, vertical, coords, pairs, count,
    out1, out2,
    ensx, field, xy, feat, weights, lifted, own1, halo1, pack1, pack2,
    local_sem, core_recv, left_recv, right_recv, core_send, left_send, right_send,
    edge_recv, edge_send, halo_recv, halo_send, one_recv, one_send, two_recv, two_send,
):
    t = lax.axis_index("space")
    m = lax.axis_index("member")
    up = lax.rem(t + 1, tiles)
    down = lax.rem(t + tiles - 1, tiles)
    last = members - 1
    nb = blocks_dev // members
    ext = nb + 2 * REACH
    width = ext * BLOCK
    core = nb * BLOCK
    cols_dev = blocks_dev * BLOCK
    levels = state.shape[0]
    groups = nb // group
    period = cols_dev * tiles // 8
    step = BLOCK // 8
    gw = group * BLOCK
    kw = (group + 2 * REACH) * BLOCK

    def cols(start, size):
        return pl.ds(pl.multiple_of(start, BLOCK), size)

    core_x = pl.ds(HALO, core)
    left_x = pl.ds(0, HALO)
    right_x = pl.ds(HALO + core, HALO)

    barrier = pltpu.get_barrier_semaphore()
    for p in range(members):
        @pl.when(p != m)
        def _(p=p):
            pl.semaphore_signal(barrier, inc=1, device_id=(t, p), device_id_type=MESH)

        @pl.when(m == 0)
        def _(p=p):
            pl.semaphore_signal(barrier, inc=1, device_id=(down, p), device_id_type=MESH)

        @pl.when(m == last)
        def _(p=p):
            pl.semaphore_signal(barrier, inc=1, device_id=(up, p), device_id_type=MESH)

    mine = m * core
    stay = [
        pltpu.make_async_copy(
            state.at[:, cols(mine, core)], field.at[:, core_x], local_sem.at[0]),
        pltpu.make_async_copy(
            coords.at[:, cols(mine, core)], xy.at[:, core_x], local_sem.at[1]),
        pltpu.make_async_copy(
            ens.at[0, :, cols(mine, core)], ensx.at[m, :, core_x], core_recv.at[m]),
    ]
    for copy in stay:
        copy.start()

    @pl.when(m > 0)
    def _():
        at = cols(mine - HALO, HALO)
        pltpu.make_async_copy(state.at[:, at], field.at[:, left_x], edge_recv.at[0]).start()
        pltpu.make_async_copy(coords.at[:, at], xy.at[:, left_x], edge_recv.at[1]).start()
        pltpu.make_async_copy(ens.at[0, :, at], ensx.at[m, :, left_x], left_recv.at[m]).start()

    @pl.when(m < last)
    def _():
        at = cols(mine + core, HALO)
        pltpu.make_async_copy(state.at[:, at], field.at[:, right_x], edge_recv.at[2]).start()
        pltpu.make_async_copy(coords.at[:, at], xy.at[:, right_x], edge_recv.at[3]).start()
        pltpu.make_async_copy(ens.at[0, :, at], ensx.at[m, :, right_x], right_recv.at[m]).start()

    pl.semaphore_wait(barrier, members + 1)

    def remote(src, dst, send, recv, where):
        return pltpu.make_async_remote_copy(
            src_ref=src, dst_ref=dst, send_sem=send, recv_sem=recv,
            device_id=where, device_id_type=MESH)

    high = pl.ds(cols_dev - HALO, HALO)
    low = pl.ds(0, HALO)
    edge_up = [
        remote(coords.at[:, high], xy.at[:, left_x], edge_send.at[1], edge_recv.at[1], (up, 0)),
        remote(state.at[:, high], field.at[:, left_x], edge_send.at[0], edge_recv.at[0], (up, 0)),
    ]
    edge_down = [
        remote(coords.at[:, low], xy.at[:, right_x], edge_send.at[3], edge_recv.at[3], (down, last)),
        remote(state.at[:, low], field.at[:, right_x], edge_send.at[2], edge_recv.at[2], (down, last)),
    ]

    @pl.when(m == last)
    def _():
        for copy in edge_up:
            copy.start()

    @pl.when(m == 0)
    def _():
        for copy in edge_down:
            copy.start()

    def core_copy(p):
        return remote(
            ens.at[0, :, pl.ds(p * core, core)], ensx.at[m, :, core_x],
            core_send.at[p], core_recv.at[m], (t, p))

    def left_copy(p):
        if p == 0:
            return remote(
                ens.at[0, :, high], ensx.at[m, :, left_x],
                left_send.at[p], left_recv.at[m], (up, 0))
        return remote(
            ens.at[0, :, pl.ds(p * core - HALO, HALO)], ensx.at[m, :, left_x],
            left_send.at[p], left_recv.at[m], (t, p))

    def right_copy(p):
        if p == last:
            return remote(
                ens.at[0, :, low], ensx.at[m, :, right_x],
                right_send.at[p], right_recv.at[m], (down, last))
        return remote(
            ens.at[0, :, pl.ds((p + 1) * core, HALO)], ensx.at[m, :, right_x],
            right_send.at[p], right_recv.at[m], (t, p))

    left_copy(0).start()
    right_copy(last).start()
    for p in range(members):
        @pl.when(p != m)
        def _(p=p):
            core_copy(p).start()
            if p != 0:
                left_copy(p).start()
            if p != last:
                right_copy(p).start()

    def arrived(ref, sem):
        pltpu.make_async_copy(ref, ref, sem).wait()

    stay[1].wait()
    arrived(xy.at[:, left_x], edge_recv.at[1])
    arrived(xy.at[:, right_x], edge_recv.at[3])
    lane = iota((1, width), 1)
    block = lane >> 7
    rel = xy[0:1, :] - step * (t * blocks_dev + m * nb - REACH + block)
    rel = jnp.where(rel < 0, rel + period, rel)
    rel = jnp.where(rel >= period, rel - period, rel)
    along = rel + step * block - (step * ext // 2 + 31)
    across = xy[1:2, :]
    square = along * along + across * across
    upper = ((square >> 7) << 7).astype(jnp.float32)
    lower = (square & 127).astype(jnp.float32)
    along = along.astype(jnp.float32)
    across = across.astype(jnp.float32)

    def rows(parts, size):
        row = iota((16, size), 0)
        table = jnp.zeros((16, size), jnp.float32)
        for i, part in enumerate(parts):
            table = jnp.where(row == i, part, table)
        return table

    blocks_x = (iota((16, width), 0) == (iota((16, width), 1) >> 7)).astype(jnp.float32)
    source = jnp.concatenate(
        [rows([along, across, upper, lower, 1.0, 1.0], width), blocks_x], axis=0)
    feat[...] = jnp.transpose(source).astype(jnp.bfloat16)

    slots = pairs.shape[1]
    first_block = m * nb + iota((16, slots), 0)
    live = iota((16, slots), 1) < count[0]
    is_dst = ((pairs[0:1, :] == first_block) & live).astype(jnp.float32).astype(jnp.bfloat16)
    is_src = (pairs[1:2, :] == first_block).astype(jnp.float32).astype(jnp.bfloat16)
    present = lax.dot_general(
        is_src, is_dst, (((1,), (1,)), ((), ())), preferred_element_type=jnp.float32)
    spread_out = (iota((16, core), 0) == (iota((16, core), 1) >> 7)).astype(jnp.float32)
    present = dot(present.astype(jnp.bfloat16), spread_out.astype(jnp.bfloat16))
    absent = jnp.where(present > 0.5, 0.0, FAR)
    own = slice(HALO, HALO + core)
    target = jnp.concatenate(
        [rows([-2.0 * along[:, own], -2.0 * across[:, own], 1.0, 1.0,
               upper[:, own], lower[:, own]], core), absent], axis=0).astype(jnp.bfloat16)

    dist = jnp.sqrt(iota((8, BLOCK), 1).astype(jnp.float32))
    table = gaspari(dist / SCALE).astype(jnp.bfloat16).astype(jnp.float32)
    table = jnp.broadcast_to(table[0:1, :], (BLOCK, BLOCK))
    for g in range(groups):
        for s in range(group + 2 * REACH):
            at = (g * group + s) * BLOCK
            d2 = dot(feat[at:at + BLOCK, :], target[:, g * gw:(g + 1) * gw])
            index = jnp.minimum(d2, 127.0).astype(jnp.int32)
            for j in range(group):
                w = jnp.take_along_axis(
                    table, index[:, j * BLOCK:(j + 1) * BLOCK], axis=1,
                    mode="promise_in_bounds")
                weights[g, s * BLOCK:(s + 1) * BLOCK, j * BLOCK:(j + 1) * BLOCK] = w.astype(
                    jnp.bfloat16)

    batch = 4 if members % 4 == 0 else 1
    tall = batch * levels
    pick = (iota((tall, levels), 0) % levels == iota((tall, levels), 1)).astype(
        jnp.float32).astype(jnp.bfloat16)
    turn = (iota((levels, tall), 1) % levels == iota((levels, tall), 0)).astype(
        jnp.float32).astype(jnp.bfloat16)
    stacked = dot(dot(pick, vertical[...]).astype(jnp.bfloat16), turn)
    same = iota((tall, tall), 0) // levels == iota((tall, tall), 1) // levels
    diagonal = jnp.where(same, stacked, 0.0).astype(jnp.bfloat16)

    def lift(at, size, values):
        for b in range(members // batch):
            schur = [
                (ensx[b * batch + i, :, at:at + size].astype(jnp.float32) * values).astype(
                    jnp.bfloat16)
                for i in range(batch)
            ]
            product = dot(diagonal, jnp.concatenate(schur, axis=0))
            lifted[b * tall:(b + 1) * tall, at:at + size] = product.astype(jnp.bfloat16)

    def summed(g):
        spread = dot(lifted[:, g * gw:g * gw + kw], weights[g])
        at = HALO + g * gw
        total = jnp.zeros((levels, gw), jnp.float32)
        for i in range(members):
            total += ensx[i, :, at:at + gw].astype(jnp.float32) * spread[
                i * levels:(i + 1) * levels, :]
        return total / (members - 1)

    edges = REACH // group if REACH % group == 0 else groups
    order = list(dict.fromkeys(
        list(range(min(edges, groups)))
        + list(range(max(groups - edges, 0), groups))
        + list(range(groups))))
    inner_first = order[::-1]

    stay[0].wait()
    arrived(field.at[:, left_x], edge_recv.at[0])
    arrived(field.at[:, right_x], edge_recv.at[2])
    for i in range(members):
        arrived(ensx.at[i, :, core_x], core_recv.at[i])
        arrived(ensx.at[i, :, left_x], left_recv.at[i])
        arrived(ensx.at[i, :, right_x], right_recv.at[i])
    for e in range(0, ext, 2) if ext % 2 == 0 else range(ext):
        size = 2 * BLOCK if ext % 2 == 0 else BLOCK
        lift(e * BLOCK, size, field[:, e * BLOCK:e * BLOCK + size])

    to_left = (jnp.where(m == 0, down, t), jnp.where(m == 0, last, m - 1))
    to_right = (jnp.where(m == last, up, t), jnp.where(m == last, 0, m + 1))
    halo_copies = [
        remote(own1.at[:, pl.ds(0, HALO)], halo1.at[1], halo_send.at[0], halo_recv.at[1], to_left),
        remote(own1.at[:, pl.ds(core - HALO, HALO)], halo1.at[0],
               halo_send.at[1], halo_recv.at[0], to_right),
    ]
    sent = [False, False]
    done = set()
    for g in order:
        result = summed(g)
        own1[:, g * gw:(g + 1) * gw] = result
        pack1[:, g * gw:(g + 1) * gw] = result.astype(jnp.bfloat16)
        done.add(g)
        for side, need in enumerate((
            {k for k in range(groups) if k * gw < HALO},
            {k for k in range(groups) if (k + 1) * gw > core - HALO},
        )):
            if not sent[side] and need <= done:
                halo_copies[side].start()
                sent[side] = True

    own_cols = cols(mine, core)

    def one_copy(p):
        return remote(pack1, out1.at[:, own_cols], one_send.at[p], one_recv.at[m], (t, p))

    def two_copy(p, g):
        return remote(
            pack2.at[:, pl.ds(g * gw, gw)], out2.at[:, cols(mine + g * gw, gw)],
            two_send.at[p, g], two_recv.at[m, g], (t, p))

    for p in range(members):
        @pl.when(p != m)
        def _(p=p):
            one_copy(p).start()
    keep1 = pltpu.make_async_copy(pack1, out1.at[:, own_cols], one_recv.at[m])
    keep1.start()

    for g in range(groups):
        lift(HALO + g * gw, gw, own1[:, g * gw:(g + 1) * gw])
    halves = [False, False]
    keep2 = []
    for g in inner_first:
        if not halves[0] and g * gw < HALO:
            halo_copies[1].wait_recv()
            lift(0, HALO, halo1[0])
            halves[0] = True
        if not halves[1] and (g + 1) * gw > core - HALO:
            halo_copies[0].wait_recv()
            lift(HALO + core, HALO, halo1[1])
            halves[1] = True
        pack2[:, g * gw:(g + 1) * gw] = summed(g).astype(jnp.bfloat16)
        for p in range(members):
            @pl.when(p != m)
            def _(p=p, g=g):
                two_copy(p, g).start()
        keep = pltpu.make_async_copy(
            pack2.at[:, pl.ds(g * gw, gw)], out2.at[:, cols(mine + g * gw, gw)],
            two_recv.at[m, g])
        keep.start()

    for side in range(2):
        halo_copies[side].wait_send()

    @pl.when(m == last)
    def _():
        for copy in edge_up:
            copy.wait_send()

    @pl.when(m == 0)
    def _():
        for copy in edge_down:
            copy.wait_send()

    left_copy(0).wait_send()
    right_copy(last).wait_send()
    for p in range(members):
        @pl.when(p != m)
        def _(p=p):
            core_copy(p).wait_send()
            if p != 0:
                left_copy(p).wait_send()
            if p != last:
                right_copy(p).wait_send()
            one_copy(p).wait_send()
            for g in range(groups):
                two_copy(p, g).wait_send()
    for i in range(members):
        arrived(out1.at[:, pl.ds(i * core, core)], one_recv.at[i])
        for g in range(groups):
            arrived(out2.at[:, pl.ds(i * core + g * gw, gw)], two_recv.at[i, g])


def on_device(tiles, members, state, ensemble, vertical, coords, pairs, pair_count):
    levels, cols_dev = state.shape
    blocks_dev = cols_dev // BLOCK
    nb = blocks_dev // members
    group = 2 if nb % 2 == 0 else 1
    groups = nb // group
    core = nb * BLOCK
    width = core + 2 * HALO
    dma = pltpu.SemaphoreType.DMA
    vmem = pl.BlockSpec(memory_space=pltpu.VMEM)
    hbm = pl.BlockSpec(memory_space=pl.ANY)
    smem = pl.BlockSpec(memory_space=pltpu.SMEM)
    first, second = pl.pallas_call(
        functools.partial(kernel, tiles, members, blocks_dev, group),
        out_shape=[jax.ShapeDtypeStruct((levels, cols_dev), jnp.bfloat16)] * 2,
        in_specs=[hbm, hbm, vmem, hbm, vmem, smem],
        out_specs=[hbm, hbm],
        scratch_shapes=[
            pltpu.VMEM((members, levels, width), jnp.bfloat16),
            pltpu.VMEM((levels, width), jnp.float32),
            pltpu.VMEM((2, width), jnp.int32),
            pltpu.VMEM((width, 32), jnp.bfloat16),
            pltpu.VMEM((groups, (group + 2 * REACH) * BLOCK, group * BLOCK), jnp.bfloat16),
            pltpu.VMEM((members * levels, width), jnp.bfloat16),
            pltpu.VMEM((levels, core), jnp.float32),
            pltpu.VMEM((2, levels, HALO), jnp.float32),
            pltpu.VMEM((levels, core), jnp.bfloat16),
            pltpu.VMEM((levels, core), jnp.bfloat16),
            dma((2,)),
            dma((members,)), dma((members,)), dma((members,)),
            dma((members,)), dma((members,)), dma((members,)),
            dma((4,)), dma((4,)),
            dma((2,)), dma((2,)),
            dma((members,)), dma((members,)),
            dma((members, groups)), dma((members, groups)),
        ],
        compiler_params=pltpu.CompilerParams(
            collective_id=0, has_side_effects=True, vmem_limit_bytes=40 * 1024 * 1024
        ),
    )(state, ensemble, vertical, coords, pairs, pair_count)
    return first.astype(jnp.float32), second.astype(jnp.float32)


def solution(mesh):
    in_specs = (
        P(None, "space"),
        P("member", None, "space"),
        P(),
        P(None, "space"),
        P(None, "space"),
        P("space"),
    )
    out_specs = (P(None, "space"), P(None, "space"))
    return jax.shard_map(
        functools.partial(on_device, mesh.shape["space"], mesh.shape["member"]),
        mesh=mesh, in_specs=in_specs, out_specs=out_specs, check_vma=False,
    )
```

```python
import functools

import jax
import jax.numpy as jnp
from jax import lax
from jax.experimental import pallas as pl
from jax.experimental.pallas import tpu as pltpu
from jax.sharding import PartitionSpec as P

BLOCK = 128
REACH = 2
SCALE = 4.0
HALO = REACH * BLOCK
FAR = 131072.0
MESH = pl.DeviceIdType.MESH


def gaspari(r):
    near = (((-0.25 * r + 0.5) * r + 0.625) * r - 5.0 / 3.0) * r * r + 1.0
    rf = jnp.maximum(r, 1.0)
    far = (
        ((((rf / 12.0 - 0.5) * rf + 0.625) * rf + 5.0 / 3.0) * rf - 5.0) * rf
        + 4.0
        - 2.0 / (3.0 * rf)
    )
    return jnp.where(r <= 1.0, near, jnp.where(r < 2.0, far, jnp.zeros_like(r)))


def iota(shape, dim):
    return lax.broadcasted_iota(jnp.int32, shape, dim)


def dot(a, b):
    return jnp.dot(a, b, preferred_element_type=jnp.float32)


def kernel(
    tiles, members, blocks_dev, group,
    state, ens, vertical_in, coords, pairs_in, count,
    out1, out2,
    vertical, pairs, ensx, field, xy, feat, weights, lifted, own1, halo1, pack1, pack2,
    local_sem, core_recv, left_recv, right_recv, core_send, left_send, right_send,
    edge_recv, edge_send, halo_recv, halo_send, one_recv, one_send, two_recv, two_send,
    one_fwd, two_fwd,
):
    t = lax.axis_index("space")
    m = lax.axis_index("member")
    up = lax.rem(t + 1, tiles)
    down = lax.rem(t + tiles - 1, tiles)
    last = members - 1
    nb = blocks_dev // members
    ext = nb + 2 * REACH
    width = ext * BLOCK
    core = nb * BLOCK
    cols_dev = blocks_dev * BLOCK
    levels = state.shape[0]
    groups = nb // group
    period = cols_dev * tiles // 8
    step = BLOCK // 8
    gw = group * BLOCK
    kw = (group + 2 * REACH) * BLOCK

    def cols(start, size):
        return pl.ds(pl.multiple_of(start, BLOCK), size)

    core_x = pl.ds(HALO, core)
    left_x = pl.ds(0, HALO)
    right_x = pl.ds(HALO + core, HALO)

    barrier = pltpu.get_barrier_semaphore()
    for p in range(members):
        @pl.when(p != m)
        def _(p=p):
            pl.semaphore_signal(barrier, inc=1, device_id=(t, p), device_id_type=MESH)

        @pl.when(m == 0)
        def _(p=p):
            pl.semaphore_signal(barrier, inc=1, device_id=(down, p), device_id_type=MESH)

        @pl.when(m == last)
        def _(p=p):
            pl.semaphore_signal(barrier, inc=1, device_id=(up, p), device_id_type=MESH)

    mine = m * core
    small = [
        pltpu.make_async_copy(pairs_in, pairs, local_sem.at[2]),
        pltpu.make_async_copy(vertical_in, vertical, local_sem.at[3]),
    ]
    stay = [
        pltpu.make_async_copy(
            state.at[:, cols(mine, core)], field.at[:, core_x], local_sem.at[0]),
        pltpu.make_async_copy(
            coords.at[:, cols(mine, core)], xy.at[:, core_x], local_sem.at[1]),
        pltpu.make_async_copy(
            ens.at[0, :, cols(mine, core)], ensx.at[m, :, core_x], core_recv.at[m]),
    ]
    stay[1].start()
    for copy in small:
        copy.start()
    stay[0].start()
    stay[2].start()

    @pl.when(m > 0)
    def _():
        at = cols(mine - HALO, HALO)
        pltpu.make_async_copy(state.at[:, at], field.at[:, left_x], edge_recv.at[0]).start()
        pltpu.make_async_copy(coords.at[:, at], xy.at[:, left_x], edge_recv.at[1]).start()
        pltpu.make_async_copy(ens.at[0, :, at], ensx.at[m, :, left_x], left_recv.at[m]).start()

    @pl.when(m < last)
    def _():
        at = cols(mine + core, HALO)
        pltpu.make_async_copy(state.at[:, at], field.at[:, right_x], edge_recv.at[2]).start()
        pltpu.make_async_copy(coords.at[:, at], xy.at[:, right_x], edge_recv.at[3]).start()
        pltpu.make_async_copy(ens.at[0, :, at], ensx.at[m, :, right_x], right_recv.at[m]).start()

    dist = jnp.sqrt(iota((8, BLOCK), 1).astype(jnp.float32))
    table = gaspari(dist / SCALE).astype(jnp.bfloat16).astype(jnp.float32)
    table = jnp.broadcast_to(table[0:1, :], (BLOCK, BLOCK))
    pl.semaphore_wait(barrier, members + 1)

    def remote(src, dst, send, recv, where):
        return pltpu.make_async_remote_copy(
            src_ref=src, dst_ref=dst, send_sem=send, recv_sem=recv,
            device_id=where, device_id_type=MESH)

    high = pl.ds(cols_dev - HALO, HALO)
    low = pl.ds(0, HALO)
    edge_up = [
        remote(coords.at[:, high], xy.at[:, left_x], edge_send.at[1], edge_recv.at[1], (up, 0)),
        remote(state.at[:, high], field.at[:, left_x], edge_send.at[0], edge_recv.at[0], (up, 0)),
    ]
    edge_down = [
        remote(coords.at[:, low], xy.at[:, right_x], edge_send.at[3], edge_recv.at[3], (down, last)),
        remote(state.at[:, low], field.at[:, right_x], edge_send.at[2], edge_recv.at[2], (down, last)),
    ]

    @pl.when(m == last)
    def _():
        for copy in edge_up:
            copy.start()

    @pl.when(m == 0)
    def _():
        for copy in edge_down:
            copy.start()

    def core_copy(p):
        return remote(
            ens.at[0, :, pl.ds(p * core, core)], ensx.at[m, :, core_x],
            core_send.at[p], core_recv.at[m], (t, p))

    def left_copy(p):
        if p == 0:
            return remote(
                ens.at[0, :, high], ensx.at[m, :, left_x],
                left_send.at[p], left_recv.at[m], (up, 0))
        return remote(
            ens.at[0, :, pl.ds(p * core - HALO, HALO)], ensx.at[m, :, left_x],
            left_send.at[p], left_recv.at[m], (t, p))

    def right_copy(p):
        if p == last:
            return remote(
                ens.at[0, :, low], ensx.at[m, :, right_x],
                right_send.at[p], right_recv.at[m], (down, last))
        return remote(
            ens.at[0, :, pl.ds((p + 1) * core, HALO)], ensx.at[m, :, right_x],
            right_send.at[p], right_recv.at[m], (t, p))

    left_copy(0).start()
    right_copy(last).start()
    for p in range(members):
        @pl.when(p != m)
        def _(p=p):
            core_copy(p).start()
            if p != 0:
                left_copy(p).start()
            if p != last:
                right_copy(p).start()

    def arrived(ref, sem):
        pltpu.make_async_copy(ref, ref, sem).wait()

    small[0].wait()
    slots = pairs.shape[1]
    first_block = m * nb + iota((16, slots), 0)
    live = iota((16, slots), 1) < count[0]
    is_dst = ((pairs[0:1, :] == first_block) & live).astype(jnp.float32).astype(jnp.bfloat16)
    is_src = (pairs[1:2, :] == first_block).astype(jnp.float32).astype(jnp.bfloat16)
    present = lax.dot_general(
        is_src, is_dst, (((1,), (1,)), ((), ())), preferred_element_type=jnp.float32)
    spread_out = (iota((16, core), 0) == (iota((16, core), 1) >> 7)).astype(jnp.float32)
    present = dot(present.astype(jnp.bfloat16), spread_out.astype(jnp.bfloat16))
    absent = jnp.where(present > 0.5, 0.0, FAR)
    small[1].wait()
    batch = 4 if members % 4 == 0 else 1
    tall = batch * levels
    pick = (iota((tall, levels), 0) % levels == iota((tall, levels), 1)).astype(
        jnp.float32).astype(jnp.bfloat16)
    turn = (iota((levels, tall), 1) % levels == iota((levels, tall), 0)).astype(
        jnp.float32).astype(jnp.bfloat16)
    stacked = dot(dot(pick, vertical[...]).astype(jnp.bfloat16), turn)
    same = iota((tall, tall), 0) // levels == iota((tall, tall), 1) // levels
    diagonal = jnp.where(same, stacked, 0.0).astype(jnp.bfloat16)

    stay[1].wait()
    arrived(xy.at[:, left_x], edge_recv.at[1])
    arrived(xy.at[:, right_x], edge_recv.at[3])
    lane = iota((1, width), 1)
    block = lane >> 7
    rel = xy[0:1, :] - step * (t * blocks_dev + m * nb - REACH + block)
    rel = jnp.where(rel < 0, rel + period, rel)
    rel = jnp.where(rel >= period, rel - period, rel)
    along = rel + step * block - (step * ext // 2 + 31)
    across = xy[1:2, :]
    square = along * along + across * across
    upper = ((square >> 7) << 7).astype(jnp.float32)
    lower = (square & 127).astype(jnp.float32)
    along = along.astype(jnp.float32)
    across = across.astype(jnp.float32)

    def rows(parts, size):
        row = iota((16, size), 0)
        table = jnp.zeros((16, size), jnp.float32)
        for i, part in enumerate(parts):
            table = jnp.where(row == i, part, table)
        return table

    blocks_x = (iota((16, width), 0) == (iota((16, width), 1) >> 7)).astype(jnp.float32)
    source = jnp.concatenate(
        [rows([along, across, upper, lower, 1.0, 1.0], width), blocks_x], axis=0)
    feat[...] = jnp.transpose(source).astype(jnp.bfloat16)

    own = slice(HALO, HALO + core)
    target = jnp.concatenate(
        [rows([-2.0 * along[:, own], -2.0 * across[:, own], 1.0, 1.0,
               upper[:, own], lower[:, own]], core), absent], axis=0).astype(jnp.bfloat16)

    for g in range(groups):
        for s in range(group + 2 * REACH):
            at = (g * group + s) * BLOCK
            d2 = dot(feat[at:at + BLOCK, :], target[:, g * gw:(g + 1) * gw])
            index = jnp.minimum(d2, 127.0).astype(jnp.int32)
            for j in range(group):
                w = jnp.take_along_axis(
                    table, index[:, j * BLOCK:(j + 1) * BLOCK], axis=1,
                    mode="promise_in_bounds")
                weights[g, s * BLOCK:(s + 1) * BLOCK, j * BLOCK:(j + 1) * BLOCK] = w.astype(
                    jnp.bfloat16)

    def lift(at, size, values):
        for b in range(members // batch):
            schur = [
                (ensx[b * batch + i, :, at:at + size].astype(jnp.float32) * values).astype(
                    jnp.bfloat16)
                for i in range(batch)
            ]
            product = dot(diagonal, jnp.concatenate(schur, axis=0))
            lifted[b * tall:(b + 1) * tall, at:at + size] = product.astype(jnp.bfloat16)

    def summed(g):
        spread = dot(lifted[:, g * gw:g * gw + kw], weights[g])
        at = HALO + g * gw
        total = jnp.zeros((levels, gw), jnp.float32)
        for i in range(members):
            total += ensx[i, :, at:at + gw].astype(jnp.float32) * spread[
                i * levels:(i + 1) * levels, :]
        return total / (members - 1)

    edges = REACH // group if REACH % group == 0 else groups
    order = list(dict.fromkeys(
        list(range(min(edges, groups)))
        + list(range(max(groups - edges, 0), groups))
        + list(range(groups))))
    inner_first = order[::-1]

    stay[0].wait()
    arrived(field.at[:, left_x], edge_recv.at[0])
    arrived(field.at[:, right_x], edge_recv.at[2])
    for i in range(members):
        arrived(ensx.at[i, :, core_x], core_recv.at[i])
        arrived(ensx.at[i, :, left_x], left_recv.at[i])
        arrived(ensx.at[i, :, right_x], right_recv.at[i])
    for e in range(0, ext, 2) if ext % 2 == 0 else range(ext):
        size = 2 * BLOCK if ext % 2 == 0 else BLOCK
        lift(e * BLOCK, size, field[:, e * BLOCK:e * BLOCK + size])

    to_left = (jnp.where(m == 0, down, t), jnp.where(m == 0, last, m - 1))
    to_right = (jnp.where(m == last, up, t), jnp.where(m == last, 0, m + 1))
    halo_copies = [
        remote(own1.at[:, pl.ds(0, HALO)], halo1.at[1], halo_send.at[0], halo_recv.at[1], to_left),
        remote(own1.at[:, pl.ds(core - HALO, HALO)], halo1.at[0],
               halo_send.at[1], halo_recv.at[0], to_right),
    ]
    sent = [False, False]
    done = set()
    for g in order:
        result = summed(g)
        own1[:, g * gw:(g + 1) * gw] = result
        pack1[:, g * gw:(g + 1) * gw] = result.astype(jnp.bfloat16)
        done.add(g)
        for side, need in enumerate((
            {k for k in range(groups) if k * gw < HALO},
            {k for k in range(groups) if (k + 1) * gw > core - HALO},
        )):
            if not sent[side] and need <= done:
                halo_copies[side].start()
                sent[side] = True

    own_cols = cols(mine, core)

    def one_copy(p):
        return remote(pack1, out1.at[:, own_cols], one_send.at[p], one_recv.at[m], (t, p))

    def two_copy(p, g):
        return remote(
            pack2.at[:, pl.ds(g * gw, gw)], out2.at[:, cols(mine + g * gw, gw)],
            two_send.at[p, g], two_recv.at[m, g], (t, p))

    sibling = m + 1 - 2 * lax.rem(m, 2)

    def abroad(p):
        return (p != m) & (lax.rem(m, 2) == p % 2)

    def one_pass(p):
        at = pl.ds(p * core, core)
        return remote(out1.at[:, at], out1.at[:, at], one_fwd.at[p], one_recv.at[p], (t, sibling))

    def two_pass(p, g):
        at = pl.ds(p * core + g * gw, gw)
        return remote(
            out2.at[:, at], out2.at[:, at], two_fwd.at[p, g], two_recv.at[p, g], (t, sibling))

    for p in range(members):
        @pl.when(abroad(p))
        def _(p=p):
            one_copy(p).start()
    one_copy(sibling).start()
    keep1 = pltpu.make_async_copy(pack1, out1.at[:, own_cols], one_recv.at[m])
    keep1.start()

    for g in range(groups):
        lift(HALO + g * gw, gw, own1[:, g * gw:(g + 1) * gw])
    halves = [False, False]
    keep2 = []
    for g in inner_first:
        if not halves[0] and g * gw < HALO:
            halo_copies[1].wait_recv()
            lift(0, HALO, halo1[0])
            halves[0] = True
        if not halves[1] and (g + 1) * gw > core - HALO:
            halo_copies[0].wait_recv()
            lift(HALO + core, HALO, halo1[1])
            halves[1] = True
        pack2[:, g * gw:(g + 1) * gw] = summed(g).astype(jnp.bfloat16)
        for p in range(members):
            @pl.when(abroad(p))
            def _(p=p, g=g):
                two_copy(p, g).start()
        two_copy(sibling, g).start()
        keep = pltpu.make_async_copy(
            pack2.at[:, pl.ds(g * gw, gw)], out2.at[:, cols(mine + g * gw, gw)],
            two_recv.at[m, g])
        keep.start()

    for p in range(members):
        @pl.when(abroad(p))
        def _(p=p):
            arrived(out1.at[:, pl.ds(p * core, core)], one_recv.at[p])
            one_pass(p).start()
    for g in inner_first:
        for p in range(members):
            @pl.when(abroad(p))
            def _(p=p, g=g):
                arrived(out2.at[:, pl.ds(p * core + g * gw, gw)], two_recv.at[p, g])
                two_pass(p, g).start()

    for side in range(2):
        halo_copies[side].wait_send()

    @pl.when(m == last)
    def _():
        for copy in edge_up:
            copy.wait_send()

    @pl.when(m == 0)
    def _():
        for copy in edge_down:
            copy.wait_send()

    left_copy(0).wait_send()
    right_copy(last).wait_send()
    for p in range(members):
        @pl.when(p != m)
        def _(p=p):
            core_copy(p).wait_send()
            if p != 0:
                left_copy(p).wait_send()
            if p != last:
                right_copy(p).wait_send()

        @pl.when(abroad(p))
        def _(p=p):
            one_copy(p).wait_send()
            one_pass(p).wait_send()
            for g in range(groups):
                two_copy(p, g).wait_send()
                two_pass(p, g).wait_send()

        @pl.when(jnp.logical_not(abroad(p)))
        def _(p=p):
            arrived(out1.at[:, pl.ds(p * core, core)], one_recv.at[p])
            for g in range(groups):
                arrived(out2.at[:, pl.ds(p * core + g * gw, gw)], two_recv.at[p, g])
    one_copy(sibling).wait_send()
    for g in range(groups):
        two_copy(sibling, g).wait_send()


def widen(first, second, out1, out2, narrow, wide, read_sem, write_sem):
    part = first.shape[1] // 3
    reads, writes = [], []
    for i, (source, out) in enumerate(((first, out1), (second, out2))):
        for k in range(3):
            at = pl.ds(k * part, part)
            reads.append(pltpu.make_async_copy(
                source.at[:, at], narrow.at[i, :, at], read_sem.at[i, k]))
            writes.append(pltpu.make_async_copy(
                wide.at[i, :, at], out.at[:, at], write_sem.at[i, k]))
            reads[-1].start()
    for n, (read, write) in enumerate(zip(reads, writes)):
        i, at = n // 3, pl.ds(n % 3 * part, part)
        read.wait()
        wide[i, :, at] = narrow[i, :, at].astype(jnp.float32)
        write.start()
    for write in writes:
        write.wait()


def on_device(tiles, members, state, ensemble, vertical, coords, pairs, pair_count):
    levels, cols_dev = state.shape
    blocks_dev = cols_dev // BLOCK
    nb = blocks_dev // members
    group = 2 if nb % 2 == 0 else 1
    groups = nb // group
    core = nb * BLOCK
    width = core + 2 * HALO
    dma = pltpu.SemaphoreType.DMA
    hbm = pl.BlockSpec(memory_space=pltpu.HBM)
    free = pl.BlockSpec(memory_space=pl.ANY)
    smem = pl.BlockSpec(memory_space=pltpu.SMEM)
    first, second = pl.pallas_call(
        functools.partial(kernel, tiles, members, blocks_dev, group),
        out_shape=[jax.ShapeDtypeStruct((levels, cols_dev), jnp.bfloat16)] * 2,
        in_specs=[hbm, hbm, hbm, hbm, hbm, smem],
        out_specs=[free, free],
        scratch_shapes=[
            pltpu.VMEM(vertical.shape, jnp.bfloat16),
            pltpu.VMEM(pairs.shape, jnp.int32),
            pltpu.VMEM((members, levels, width), jnp.bfloat16),
            pltpu.VMEM((levels, width), jnp.float32),
            pltpu.VMEM((2, width), jnp.int32),
            pltpu.VMEM((width, 32), jnp.bfloat16),
            pltpu.VMEM((groups, (group + 2 * REACH) * BLOCK, group * BLOCK), jnp.bfloat16),
            pltpu.VMEM((members * levels, width), jnp.bfloat16),
            pltpu.VMEM((levels, core), jnp.float32),
            pltpu.VMEM((2, levels, HALO), jnp.float32),
            pltpu.VMEM((levels, core), jnp.bfloat16),
            pltpu.VMEM((levels, core), jnp.bfloat16),
            dma((4,)),
            dma((members,)), dma((members,)), dma((members,)),
            dma((members,)), dma((members,)), dma((members,)),
            dma((4,)), dma((4,)),
            dma((2,)), dma((2,)),
            dma((members,)), dma((members,)),
            dma((members, groups)), dma((members, groups)),
            dma((members,)), dma((members, groups)),
        ],
        compiler_params=pltpu.CompilerParams(
            collective_id=0, has_side_effects=True, vmem_limit_bytes=60 * 1024 * 1024
        ),
    )(state, ensemble, vertical, coords, pairs, pair_count)
    return pl.pallas_call(
        widen,
        out_shape=[jax.ShapeDtypeStruct((levels, cols_dev), jnp.float32)] * 2,
        in_specs=[hbm, hbm],
        out_specs=[hbm, hbm],
        scratch_shapes=[
            pltpu.VMEM((2, levels, cols_dev), jnp.bfloat16),
            pltpu.VMEM((2, levels, cols_dev), jnp.float32),
            dma((2, 3)), dma((2, 3)),
        ],
        compiler_params=pltpu.CompilerParams(vmem_limit_bytes=60 * 1024 * 1024),
    )(first, second)


def solution(mesh):
    in_specs = (
        P(None, "space"),
        P("member", None, "space"),
        P(),
        P(None, "space"),
        P(None, "space"),
        P("space"),
    )
    out_specs = (P(None, "space"), P(None, "space"))
    return jax.shard_map(
        functools.partial(on_device, mesh.shape["space"], mesh.shape["member"]),
        mesh=mesh, in_specs=in_specs, out_specs=out_specs, check_vma=False,
    )
```

```python
import functools

import jax
import jax.numpy as jnp
from jax import lax
from jax.experimental import pallas as pl
from jax.experimental.pallas import tpu as pltpu
from jax.sharding import PartitionSpec as P

BLOCK = 128
REACH = 2
SCALE = 4.0


def CHUNKS(groups):
    return [(1, groups - 2), (groups - 1, 1), (0, 1)] if groups > 2 else [(0, groups)]


HALO = REACH * BLOCK
FAR = 131072.0
MESH = pl.DeviceIdType.MESH


def gaspari(r):
    near = (((-0.25 * r + 0.5) * r + 0.625) * r - 5.0 / 3.0) * r * r + 1.0
    rf = jnp.maximum(r, 1.0)
    far = (
        ((((rf / 12.0 - 0.5) * rf + 0.625) * rf + 5.0 / 3.0) * rf - 5.0) * rf
        + 4.0
        - 2.0 / (3.0 * rf)
    )
    return jnp.where(r <= 1.0, near, jnp.where(r < 2.0, far, jnp.zeros_like(r)))


def iota(shape, dim):
    return lax.broadcasted_iota(jnp.int32, shape, dim)


def dot(a, b):
    return jnp.dot(a, b, preferred_element_type=jnp.float32)


def kernel(
    tiles, members, blocks_dev, group,
    state, ens, vertical_in, coords, pairs_in, count,
    out1, out2,
    vertical, pairs, ensx, field, xy, feat, weights, lifted, own1, halo1, pack1, pack2,
    local_sem, core_recv, left_recv, right_recv, core_send, left_send, right_send,
    edge_recv, edge_send, halo_recv, halo_send, one_recv, one_send, two_recv, two_send,
    one_fwd, two_fwd,
):
    t = lax.axis_index("space")
    m = lax.axis_index("member")
    up = lax.rem(t + 1, tiles)
    down = lax.rem(t + tiles - 1, tiles)
    last = members - 1
    nb = blocks_dev // members
    ext = nb + 2 * REACH
    width = ext * BLOCK
    core = nb * BLOCK
    cols_dev = blocks_dev * BLOCK
    levels = state.shape[0]
    groups = nb // group
    period = cols_dev * tiles // 8
    step = BLOCK // 8
    gw = group * BLOCK
    kw = (group + 2 * REACH) * BLOCK

    def cols(start, size):
        return pl.ds(pl.multiple_of(start, BLOCK), size)

    core_x = pl.ds(HALO, core)
    left_x = pl.ds(0, HALO)
    right_x = pl.ds(HALO + core, HALO)

    barrier = pltpu.get_barrier_semaphore()
    for p in range(members):
        @pl.when(p != m)
        def _(p=p):
            pl.semaphore_signal(barrier, inc=1, device_id=(t, p), device_id_type=MESH)

        @pl.when(m == 0)
        def _(p=p):
            pl.semaphore_signal(barrier, inc=1, device_id=(down, p), device_id_type=MESH)

        @pl.when(m == last)
        def _(p=p):
            pl.semaphore_signal(barrier, inc=1, device_id=(up, p), device_id_type=MESH)

    def inside(p):
        lo, hi = max(p * core - HALO, 0), min((p + 1) * core + HALO, cols_dev)
        return pl.ds(lo, hi - lo), pl.ds(lo - (p * core - HALO), hi - lo)

    reach = group + 2 * REACH
    if group == REACH and ext > 2 * reach:
        pieces = [(0, reach), (ext - reach, reach), (reach, ext - 2 * reach)]
    else:
        pieces = [(0, ext)]
    early = len(pieces) - 1

    def inside_piece(p, k):
        start = p * core - HALO
        lo = max(start + pieces[k][0] * BLOCK, 0)
        hi = min(start + (pieces[k][0] + pieces[k][1]) * BLOCK, cols_dev)
        return pl.ds(lo, hi - lo), pl.ds(lo - start, hi - lo)

    mine = m * core
    small = [
        pltpu.make_async_copy(pairs_in, pairs, local_sem.at[2]),
        pltpu.make_async_copy(vertical_in, vertical, local_sem.at[3]),
    ]

    def stay(p):
        there, here = inside(p)
        return [
            pltpu.make_async_copy(coords.at[:, there], xy.at[:, here], local_sem.at[1]),
            pltpu.make_async_copy(state.at[:, there], field.at[:, here], local_sem.at[0]),
        ] + [
            pltpu.make_async_copy(
                ens.at[0, :, inside_piece(p, k)[0]], ensx.at[m, :, inside_piece(p, k)[1]],
                core_recv.at[m, k])
            for k in range(len(pieces))
        ]

    for p in range(members):
        @pl.when(p == m)
        def _(p=p):
            for copy in stay(p):
                copy.start()
    for copy in small:
        copy.start()

    dist = jnp.sqrt(iota((8, BLOCK), 1).astype(jnp.float32))
    table = gaspari(dist / SCALE).astype(jnp.bfloat16).astype(jnp.float32)
    table = jnp.broadcast_to(table[0:1, :], (BLOCK, BLOCK))
    pl.semaphore_wait(barrier, members + 1)

    def remote(src, dst, send, recv, where):
        return pltpu.make_async_remote_copy(
            src_ref=src, dst_ref=dst, send_sem=send, recv_sem=recv,
            device_id=where, device_id_type=MESH)

    high = pl.ds(cols_dev - HALO, HALO)
    low = pl.ds(0, HALO)
    edge_up = [
        remote(coords.at[:, high], xy.at[:, left_x], edge_send.at[1], edge_recv.at[1], (up, 0)),
        remote(state.at[:, high], field.at[:, left_x], edge_send.at[0], edge_recv.at[0], (up, 0)),
    ]
    edge_down = [
        remote(coords.at[:, low], xy.at[:, right_x], edge_send.at[3], edge_recv.at[3], (down, last)),
        remote(state.at[:, low], field.at[:, right_x], edge_send.at[2], edge_recv.at[2], (down, last)),
    ]

    @pl.when(m == last)
    def _():
        for copy in edge_up:
            copy.start()

    @pl.when(m == 0)
    def _():
        for copy in edge_down:
            copy.start()

    def core_copy(p, k):
        there, here = inside_piece(p, k)
        return remote(
            ens.at[0, :, there], ensx.at[m, :, here],
            core_send.at[p, k], core_recv.at[m, k], (t, p))

    left_copy = remote(
        ens.at[0, :, high], ensx.at[m, :, left_x], left_send.at[0], left_recv.at[m], (up, 0))
    right_copy = remote(
        ens.at[0, :, low], ensx.at[m, :, right_x], right_send.at[0], right_recv.at[m], (down, last))
    left_copy.start()
    right_copy.start()
    for k in range(len(pieces)):
        for p in range(members):
            @pl.when(p != m)
            def _(p=p, k=k):
                core_copy(p, k).start()

    def arrived(ref, sem):
        pltpu.make_async_copy(ref, ref, sem).wait()

    small[0].wait()
    slots = pairs.shape[1]
    first_block = m * nb + iota((16, slots), 0)
    live = iota((16, slots), 1) < count[0]
    is_dst = ((pairs[0:1, :] == first_block) & live).astype(jnp.float32).astype(jnp.bfloat16)
    is_src = (pairs[1:2, :] == first_block).astype(jnp.float32).astype(jnp.bfloat16)
    present = lax.dot_general(
        is_src, is_dst, (((1,), (1,)), ((), ())), preferred_element_type=jnp.float32)
    spread_out = (iota((16, core), 0) == (iota((16, core), 1) >> 7)).astype(jnp.float32)
    present = dot(present.astype(jnp.bfloat16), spread_out.astype(jnp.bfloat16))
    absent = jnp.where(present > 0.5, 0.0, FAR)
    small[1].wait()
    batch = 4 if members % 4 == 0 else 1
    tall = batch * levels
    pick = (iota((tall, levels), 0) % levels == iota((tall, levels), 1)).astype(
        jnp.float32).astype(jnp.bfloat16)
    turn = (iota((levels, tall), 1) % levels == iota((levels, tall), 0)).astype(
        jnp.float32).astype(jnp.bfloat16)
    stacked = dot(dot(pick, vertical[...]).astype(jnp.bfloat16), turn)
    same = iota((tall, tall), 0) // levels == iota((tall, tall), 1) // levels
    diagonal = jnp.where(same, stacked, 0.0).astype(jnp.bfloat16)

    for p in range(members):
        @pl.when(p == m)
        def _(p=p):
            stay(p)[0].wait()

    @pl.when(m == 0)
    def _():
        arrived(xy.at[:, left_x], edge_recv.at[1])

    @pl.when(m == last)
    def _():
        arrived(xy.at[:, right_x], edge_recv.at[3])

    lane = iota((1, width), 1)
    block = lane >> 7
    rel = xy[0:1, :] - step * (t * blocks_dev + m * nb - REACH + block)
    rel = jnp.where(rel < 0, rel + period, rel)
    rel = jnp.where(rel >= period, rel - period, rel)
    along = rel + step * block - (step * ext // 2 + 31)
    across = xy[1:2, :]
    square = along * along + across * across
    upper = ((square >> 7) << 7).astype(jnp.float32)
    lower = (square & 127).astype(jnp.float32)
    along = along.astype(jnp.float32)
    across = across.astype(jnp.float32)

    def rows(parts, size):
        row = iota((16, size), 0)
        table = jnp.zeros((16, size), jnp.float32)
        for i, part in enumerate(parts):
            table = jnp.where(row == i, part, table)
        return table

    blocks_x = (iota((16, width), 0) == (iota((16, width), 1) >> 7)).astype(jnp.float32)
    source = jnp.concatenate(
        [rows([along, across, upper, lower, 1.0, 1.0], width), blocks_x], axis=0)
    feat[...] = jnp.transpose(source).astype(jnp.bfloat16)

    own = slice(HALO, HALO + core)
    target = jnp.concatenate(
        [rows([-2.0 * along[:, own], -2.0 * across[:, own], 1.0, 1.0,
               upper[:, own], lower[:, own]], core), absent], axis=0).astype(jnp.bfloat16)

    for g in range(groups):
        for s in range(group + 2 * REACH):
            at = (g * group + s) * BLOCK
            d2 = dot(feat[at:at + BLOCK, :], target[:, g * gw:(g + 1) * gw])
            index = jnp.minimum(d2, 127.0).astype(jnp.int32)
            for j in range(group):
                w = jnp.take_along_axis(
                    table, index[:, j * BLOCK:(j + 1) * BLOCK], axis=1,
                    mode="promise_in_bounds")
                weights[g, s * BLOCK:(s + 1) * BLOCK, j * BLOCK:(j + 1) * BLOCK] = w.astype(
                    jnp.bfloat16)

    def lift(at, size, values):
        for b in range(members // batch):
            schur = [
                (ensx[b * batch + i, :, at:at + size].astype(jnp.float32) * values).astype(
                    jnp.bfloat16)
                for i in range(batch)
            ]
            product = dot(diagonal, jnp.concatenate(schur, axis=0))
            lifted[b * tall:(b + 1) * tall, at:at + size] = product.astype(jnp.bfloat16)

    def summed(g):
        spread = dot(lifted[:, g * gw:g * gw + kw], weights[g])
        at = HALO + g * gw
        total = jnp.zeros((levels, gw), jnp.float32)
        for i in range(members):
            total += ensx[i, :, at:at + gw].astype(jnp.float32) * spread[
                i * levels:(i + 1) * levels, :]
        return total / (members - 1)

    edges = REACH // group if REACH % group == 0 else groups
    order = list(dict.fromkeys(
        list(range(min(edges, groups)))
        + list(range(max(groups - edges, 0), groups))
        + list(range(groups))))
    inner_first = order[::-1]
    chunks = CHUNKS(groups)

    def chunk(k):
        return chunks[k][0] * gw, chunks[k][1] * gw


    for p in range(members):
        @pl.when(p == m)
        def _(p=p):
            arrived(field.at[:, inside(p)[1]], local_sem.at[0])

    def piece_arrived(k):
        for p in range(members):
            @pl.when(p == m)
            def _(p=p):
                for i in range(members):
                    arrived(ensx.at[i, :, inside_piece(p, k)[1]], core_recv.at[i, k])

    def lift_piece(k):
        start, many = pieces[k]
        span = 2 if many % 2 == 0 else 1
        for e in range(start, start + many, span):
            at = e * BLOCK
            lift(at, span * BLOCK, field[:, at:at + span * BLOCK])

    for k in range(max(early, 1)):
        piece_arrived(k)

    @pl.when(m == 0)
    def _():
        arrived(field.at[:, left_x], edge_recv.at[0])
        for i in range(members):
            arrived(ensx.at[i, :, left_x], left_recv.at[i])

    @pl.when(m == last)
    def _():
        arrived(field.at[:, right_x], edge_recv.at[2])
        for i in range(members):
            arrived(ensx.at[i, :, right_x], right_recv.at[i])

    for k in range(max(early, 1)):
        lift_piece(k)

    to_left = (jnp.where(m == 0, down, t), jnp.where(m == 0, last, m - 1))
    to_right = (jnp.where(m == last, up, t), jnp.where(m == last, 0, m + 1))
    halo_copies = [
        remote(pack1.at[:, pl.ds(0, HALO)], halo1.at[1], halo_send.at[0], halo_recv.at[1], to_left),
        remote(pack1.at[:, pl.ds(core - HALO, HALO)], halo1.at[0],
               halo_send.at[1], halo_recv.at[0], to_right),
    ]
    sent = [False, False]
    done = set()
    for n, g in enumerate(order):
        if early and n == 2:
            piece_arrived(early)
            lift_piece(early)
        result = summed(g)
        own1[:, g * gw:(g + 1) * gw] = result
        pack1[:, g * gw:(g + 1) * gw] = result.astype(jnp.bfloat16)
        done.add(g)
        for side, need in enumerate((
            {k for k in range(groups) if k * gw < HALO},
            {k for k in range(groups) if (k + 1) * gw > core - HALO},
        )):
            if not sent[side] and need <= done:
                halo_copies[side].start()
                sent[side] = True

    own_cols = cols(mine, core)

    def one_copy(p):
        return remote(pack1, out1.at[:, own_cols], one_send.at[p], one_recv.at[m], (t, p))

    def two_copy(p, k):
        at, size = chunk(k)
        return remote(
            pack2.at[:, pl.ds(at, size)], out2.at[:, cols(mine + at, size)],
            two_send.at[p, k], two_recv.at[m, k], (t, p))

    sibling = m + 1 - 2 * lax.rem(m, 2)

    def abroad(p):
        return (p != m) & (lax.rem(m, 2) == p % 2)

    def relayed(k):
        return len(chunks) == 1 or k == 0

    def reached(p, k):
        return abroad(p) if relayed(k) else (p != m) & (p != sibling)

    def one_pass(p):
        at = pl.ds(p * core, core)
        return remote(out1.at[:, at], out1.at[:, at], one_fwd.at[p], one_recv.at[p], (t, sibling))

    def two_at(p, k):
        at, size = chunk(k)
        return out2.at[:, pl.ds(p * core + at, size)]

    def two_pass(p, k):
        return remote(
            two_at(p, k), two_at(p, k), two_fwd.at[p, k], two_recv.at[p, k], (t, sibling))

    for p in range(members):
        @pl.when(abroad(p))
        def _(p=p):
            one_copy(p).start()
    one_copy(sibling).start()
    keep1 = pltpu.make_async_copy(pack1, out1.at[:, own_cols], one_recv.at[m])
    keep1.start()

    for g in range(groups):
        lift(HALO + g * gw, gw, own1[:, g * gw:(g + 1) * gw])
    halves = [False, False]
    ready, sent2 = set(), []
    for g in inner_first:
        if not halves[0] and g * gw < HALO:
            halo_copies[1].wait_recv()
            lift(0, HALO, halo1[0].astype(jnp.float32))
            halves[0] = True
        if not halves[1] and (g + 1) * gw > core - HALO:
            halo_copies[0].wait_recv()
            lift(HALO + core, HALO, halo1[1].astype(jnp.float32))
            halves[1] = True
        pack2[:, g * gw:(g + 1) * gw] = summed(g).astype(jnp.bfloat16)
        ready.add(g)
        for k, (start, many) in enumerate(chunks):
            if k in sent2 or not set(range(start, start + many)) <= ready:
                continue
            sent2.append(k)
            for p in range(members):
                @pl.when(reached(p, k))
                def _(p=p, k=k):
                    two_copy(p, k).start()
            two_copy(sibling, k).start()
            at, size = chunk(k)
            pltpu.make_async_copy(
                pack2.at[:, pl.ds(at, size)], out2.at[:, cols(mine + at, size)],
                two_recv.at[m, k]).start()

    for p in range(members):
        @pl.when(abroad(p))
        def _(p=p):
            arrived(out1.at[:, pl.ds(p * core, core)], one_recv.at[p])
            one_pass(p).start()
    for k in filter(relayed, sent2):
        for p in range(members):
            @pl.when(abroad(p))
            def _(p=p, k=k):
                arrived(two_at(p, k), two_recv.at[p, k])
                two_pass(p, k).start()

    for side in range(2):
        halo_copies[side].wait_send()

    @pl.when(m == last)
    def _():
        for copy in edge_up:
            copy.wait_send()

    @pl.when(m == 0)
    def _():
        for copy in edge_down:
            copy.wait_send()

    left_copy.wait_send()
    right_copy.wait_send()
    for p in range(members):
        @pl.when(p != m)
        def _(p=p):
            for k in range(len(pieces)):
                core_copy(p, k).wait_send()

        @pl.when(abroad(p))
        def _(p=p):
            one_copy(p).wait_send()
            one_pass(p).wait_send()
            for k in filter(relayed, sent2):
                two_pass(p, k).wait_send()

        @pl.when(jnp.logical_not(abroad(p)))
        def _(p=p):
            arrived(out1.at[:, pl.ds(p * core, core)], one_recv.at[p])
            for k in filter(relayed, sent2):
                arrived(two_at(p, k), two_recv.at[p, k])

        for k in sent2:
            @pl.when(reached(p, k))
            def _(p=p, k=k):
                two_copy(p, k).wait_send()

            if not relayed(k):
                arrived(two_at(p, k), two_recv.at[p, k])
    one_copy(sibling).wait_send()
    for k in sent2:
        two_copy(sibling, k).wait_send()


def widen(first, second, out1, out2, narrow, wide, read_sem, write_sem):
    part = first.shape[1] // 3
    reads, writes = [], []
    for i, (source, out) in enumerate(((first, out1), (second, out2))):
        for k in range(3):
            at = pl.ds(k * part, part)
            reads.append(pltpu.make_async_copy(
                source.at[:, at], narrow.at[i, :, at], read_sem.at[i, k]))
            writes.append(pltpu.make_async_copy(
                wide.at[i, :, at], out.at[:, at], write_sem.at[i, k]))
            reads[-1].start()
    for n, (read, write) in enumerate(zip(reads, writes)):
        i, at = n // 3, pl.ds(n % 3 * part, part)
        read.wait()
        wide[i, :, at] = narrow[i, :, at].astype(jnp.float32)
        write.start()
    for write in writes:
        write.wait()


def on_device(tiles, members, state, ensemble, vertical, coords, pairs, pair_count):
    levels, cols_dev = state.shape
    blocks_dev = cols_dev // BLOCK
    nb = blocks_dev // members
    group = 2 if nb % 2 == 0 else 1
    groups = nb // group
    core = nb * BLOCK
    width = core + 2 * HALO
    dma = pltpu.SemaphoreType.DMA
    hbm = pl.BlockSpec(memory_space=pltpu.HBM)
    free = pl.BlockSpec(memory_space=pl.ANY)
    smem = pl.BlockSpec(memory_space=pltpu.SMEM)
    first, second = pl.pallas_call(
        functools.partial(kernel, tiles, members, blocks_dev, group),
        out_shape=[jax.ShapeDtypeStruct((levels, cols_dev), jnp.bfloat16)] * 2,
        in_specs=[hbm, hbm, hbm, hbm, hbm, smem],
        out_specs=[free, free],
        scratch_shapes=[
            pltpu.VMEM(vertical.shape, jnp.bfloat16),
            pltpu.VMEM(pairs.shape, jnp.int32),
            pltpu.VMEM((members, levels, width), jnp.bfloat16),
            pltpu.VMEM((levels, width), jnp.float32),
            pltpu.VMEM((2, width), jnp.int32),
            pltpu.VMEM((width, 32), jnp.bfloat16),
            pltpu.VMEM((groups, (group + 2 * REACH) * BLOCK, group * BLOCK), jnp.bfloat16),
            pltpu.VMEM((members * levels, width), jnp.bfloat16),
            pltpu.VMEM((levels, core), jnp.float32),
            pltpu.VMEM((2, levels, HALO), jnp.bfloat16),
            pltpu.VMEM((levels, core), jnp.bfloat16),
            pltpu.VMEM((levels, core), jnp.bfloat16),
            dma((4,)),
            dma((members, 3)), dma((members,)), dma((members,)),
            dma((members, 3)), dma((members,)), dma((members,)),
            dma((4,)), dma((4,)),
            dma((2,)), dma((2,)),
            dma((members,)), dma((members,)),
            dma((members, groups)), dma((members, groups)),
            dma((members,)), dma((members, groups)),
        ],
        compiler_params=pltpu.CompilerParams(
            collective_id=0, has_side_effects=True, vmem_limit_bytes=60 * 1024 * 1024
        ),
    )(state, ensemble, vertical, coords, pairs, pair_count)
    return pl.pallas_call(
        widen,
        out_shape=[jax.ShapeDtypeStruct((levels, cols_dev), jnp.float32)] * 2,
        in_specs=[hbm, hbm],
        out_specs=[hbm, hbm],
        scratch_shapes=[
            pltpu.VMEM((2, levels, cols_dev), jnp.bfloat16),
            pltpu.VMEM((2, levels, cols_dev), jnp.float32),
            dma((2, 3)), dma((2, 3)),
        ],
        compiler_params=pltpu.CompilerParams(vmem_limit_bytes=60 * 1024 * 1024),
    )(first, second)


def solution(mesh):
    in_specs = (
        P(None, "space"),
        P("member", None, "space"),
        P(),
        P(None, "space"),
        P(None, "space"),
        P("space"),
    )
    out_specs = (P(None, "space"), P(None, "space"))
    return jax.shard_map(
        functools.partial(on_device, mesh.shape["space"], mesh.shape["member"]),
        mesh=mesh, in_specs=in_specs, out_specs=out_specs, check_vma=False,
    )
```
